32 devices in a mesh: dp: 4 (over y, core), tensor: 2 (over x), expert: 4 (over z).
Axes of the slice: x: 2, y: 2, z: 4, core: 2. Of those that a mesh axis runs over, the one named last changes fastest.
Arguments:
- tokens: bfloat16 [512, 4096], P(('tensor', 'expert'), 'dp'), may hold values from -6 to 6
- routes: int32 [512, 8], P(('tensor', 'expert')), may hold values from 0 to 63, as said below
- gate_probs: float32 [512, 8], P(('tensor', 'expert')), may hold values from 0.05 to 0.5
- w_gate: bfloat16 [64, 4096, 1536], P(('tensor', 'expert'), 'dp'), may hold values from -0.09375 to 0.09375
- w_up: bfloat16 [64, 4096, 1536], P(('tensor', 'expert'), 'dp'), may hold values from -0.09375 to 0.09375
- w_down: bfloat16 [64, 1536, 4096], P(('tensor', 'expert'), None, 'dp'), may hold values from -0.15625 to 0.15625
Outputs:
- combined: bfloat16 [512, 4096], P(('tensor', 'expert'), 'dp')
The draws below stay inside these ranges and needn't reach their ends.
Inputs may be any that keep to these rules, and one draw needn't show every extreme that they name: `routes`: each token names 8 different experts. In each aligned block of 64 rows no expert is named more than 16 times, and in every block some expert is named exactly 16 times.
All inputs are finite; a program needn't handle non-finite values.
Results may differ from the reference program's by a relative error of at most 0.019.
Values may be sent and summed in bfloat16 or wider, within the bound.
A program may use at most 192 MiB of HBM per device.

```python
import math
import jax
import jax.numpy as jnp
from jax import lax

D = 4096
FF = 1536
EXPERTS = 64
TOPK = 8
TOK_GRP = 64
TOKENS = 512
EXP_CAP = 16
DBLK = 1024
N_DP = 4


def draw_routes(key, part):
    key = jax.random.fold_in(key, 7)
    hot_key, pick_key, block_key = jax.random.split(key, 3)
    block_count = TOKENS // TOK_GRP
    base_load = TOK_GRP * TOPK // EXPERTS
    group_size = EXPERTS // 8
    expert_ids = jnp.arange(EXPERTS, dtype=jnp.int32)
    hotness = jax.random.randint(hot_key, (EXPERTS,), 0, 4)
    hottest = jax.random.randint(pick_key, (), 0, EXPERTS)
    hotness = hotness.at[hottest].set(8)

    def one_block(sub_key):
        noise_key, move_key, rank_key, token_key = jax.random.split(sub_key, 4)
        noise_draw = jax.random.randint(noise_key, (EXPERTS,), 0, 1024)
        score_value = (hotness * 1024 + noise_draw) * EXPERTS + expert_ids
        sort_order = jnp.argsort(-score_value)
        move_sizes = jax.random.randint(move_key, (group_size,), 1, base_load + 1)
        change = jnp.zeros((EXPERTS,), jnp.int32)
        change = change.at[sort_order[:group_size]].add(base_load)
        change = change.at[sort_order[group_size:2 * group_size]].add(move_sizes)
        change = change.at[sort_order[EXPERTS - 2 * group_size:EXPERTS - group_size]].add(-move_sizes)
        change = change.at[sort_order[EXPERTS - group_size:]].add(-base_load)
        load_count = base_load + change
        rank_value = jax.random.permutation(rank_key, EXPERTS).astype(jnp.int32)
        rounds = jnp.arange(2 * base_load, dtype=jnp.int32)[:, None]
        keys_all = jnp.where(rounds < load_count[None, :], rounds * EXPERTS + rank_value[None, :], (2 * base_load + rounds) * EXPERTS + expert_ids[None, :])
        chosen = jnp.argsort(keys_all.reshape(-1))[:TOK_GRP * TOPK]
        token_table = (chosen % EXPERTS).reshape(TOK_GRP, TOPK)
        token_order = jax.random.permutation(token_key, TOK_GRP)
        return token_table[token_order]
    blocks = jax.vmap(one_block)(jax.random.split(block_key, block_count))
    return blocks.reshape(TOKENS, TOPK).astype(jnp.int32)


def levels(own_key, shape, shards, low, largest):
    level = 1.0
    for axis_at, parts in shards:
        heights = jax.random.uniform(jax.random.fold_in(jax.random.fold_in(own_key, 6), axis_at), (parts,), jnp.float32, low / len(shards), largest / len(shards))
        level = level * jnp.repeat(jnp.exp(heights), shape[axis_at] // parts).reshape((-1,) + (1,) * (len(shape) - 1 - axis_at))
    return level


def scatter_about(own_key, extent, spread, limit, pieces=(), kind=jnp.bfloat16):
    loudness = levels(own_key, extent, pieces, -0.22, 0.18) if pieces else 1.0
    drawn = jax.random.normal(own_key, extent, jnp.float32) * spread * loudness
    return jnp.minimum(jnp.maximum(drawn, -limit), limit).astype(kind)


def setup_inputs(seed: int = 0) -> dict:
    streams_of = jax.random.split(jax.random.key(seed), 7)
    tokens = scatter_about(streams_of[0], (TOKENS, D), 1.0, 6.0, ((0, 8), (1, 4)))
    routes = draw_routes(jax.random.fold_in(streams_of[6], 71), 0)
    gate_probs = jnp.clip(jnp.exp(math.log(0.5) - 2.3025851 * jax.random.uniform(streams_of[2], (TOKENS, TOPK), jnp.float32) ** levels(streams_of[2], (TOKENS, TOPK), ((0, 8),), -0.2, 0.2)), 0.05, 0.5)
    w_gate = scatter_about(streams_of[3], (EXPERTS, D, FF), D ** -0.5, 0.09375, ((0, 8), (1, 4)))
    w_up = scatter_about(streams_of[4], (EXPERTS, D, FF), D ** -0.5, 0.09375, ((0, 8), (1, 4)))
    w_down = scatter_about(streams_of[5], (EXPERTS, FF, D), FF ** -0.5, 0.15625, ((0, 8), (2, 4)))
    return {"tokens": tokens, "routes": routes, "gate_probs": gate_probs, "w_gate": w_gate, "w_up": w_up, "w_down": w_down}


def reference(tokens, routes, gate_probs, w_gate, w_up, w_down):
    flat_routes = routes.reshape(-1).astype(jnp.int32)
    assignments = flat_routes.shape[0]
    expert_ids = jnp.arange(EXPERTS, dtype=jnp.int32)
    counts = jnp.sum((flat_routes[:, None] == expert_ids[None, :]).astype(jnp.int32), axis=0)
    starts = jnp.cumsum(counts) - counts
    sort_order = jnp.argsort(flat_routes, stable=True).astype(jnp.int32)
    weight_flat = gate_probs.reshape(-1)
    capacity_all = (TOKENS // TOK_GRP) * EXP_CAP
    slot_ids = jnp.arange(capacity_all, dtype=jnp.int32)

    def per_expert(combined, carried):
        expert, gate_matrix, up_matrix, down_matrix = carried
        is_valid = slot_ids < counts[expert]
        where_at = jnp.clip(starts[expert] + slot_ids, 0, assignments - 1)
        assign_ids = sort_order[where_at]
        token_ids = assign_ids // TOPK
        picked = jnp.where(is_valid[:, None], tokens[token_ids], jnp.zeros((), tokens.dtype))
        gate_pre = jnp.zeros((capacity_all, FF), jnp.float32)
        up_pre = jnp.zeros((capacity_all, FF), jnp.float32)
        for block_index in range(N_DP):
            first = block_index * DBLK
            gate_part = jnp.dot(picked[:, first:first + DBLK], gate_matrix[first:first + DBLK], preferred_element_type=jnp.float32)
            up_part = jnp.dot(picked[:, first:first + DBLK], up_matrix[first:first + DBLK], preferred_element_type=jnp.float32)
            gate_pre = gate_pre + lax.optimization_barrier(gate_part.astype(jnp.bfloat16)).astype(jnp.float32)
            up_pre = up_pre + lax.optimization_barrier(up_part.astype(jnp.bfloat16)).astype(jnp.float32)
        hidden = (jax.nn.silu(gate_pre) * up_pre).astype(jnp.bfloat16)
        expert_out = jnp.dot(hidden, down_matrix, preferred_element_type=jnp.float32).astype(jnp.bfloat16)
        weight_row = jnp.where(is_valid, weight_flat[assign_ids], jnp.zeros((), weight_flat.dtype))
        combined = combined.at[token_ids].add(weight_row[:, None] * expert_out.astype(jnp.float32))
        return combined, None

    start_sum = jnp.zeros((TOKENS, D), jnp.float32)
    combined, _ = lax.scan(per_expert, start_sum, (expert_ids, w_gate, w_up, w_down))
    return combined.astype(jnp.bfloat16)
```

```python
import functools

import jax
import jax.numpy as jnp
from jax import lax
from jax.experimental import pallas as pl
from jax.experimental.pallas import tpu as pltpu
from jax.sharding import PartitionSpec as P

BF = jnp.bfloat16
F32 = jnp.float32
CORES = 2


def cut(total, tile):
    return [(at, min(tile, total - at)) for at in range(0, total, tile)]


def experts_kernel(
    n_y, base, pool, unit, full_rows,
    tok_ref, rank_ref, prob_ref, prow_ref, pcol_ref, wg_hbm, wu_hbm, wd_hbm,
    out_ref,
    wg, wu, wd, part, over, sib, red, yrec, hid, eo, gmat,
    gsem, usem, dsem, s1s, s1r, y1s, y1r, y2s, y2r, s2s, s2r,
):
    n_exp, db, ff = wg_hbm.shape
    tok_count = tok_ref.shape[0]
    slots, dslots = wg.shape[0], wd.shape[0]
    per = base // unit
    units = part.shape[0]
    pool_units = pool // unit
    spill = full_rows - base
    me = lax.axis_index("dp")
    core = lax.rem(me, CORES)
    row = me // CORES
    sibling = row * CORES + (1 - core)

    def y_peer(k):
        return lax.rem(row + k, n_y) * CORES + core

    def load_gu(e):
        at = lax.rem(e, slots)
        return (
            pltpu.make_async_copy(wg_hbm.at[e], wg.at[at], gsem.at[at]),
            pltpu.make_async_copy(wu_hbm.at[e], wu.at[at], usem.at[at]),
        )

    def load_d(e):
        at = lax.rem(e, dslots)
        return pltpu.make_async_copy(wd_hbm.at[e], wd.at[at], dsem.at[at])

    def send_half(u):
        return pltpu.make_async_remote_copy(
            part.at[u, 1 - core], sib.at[u], s1s.at[u], s1r.at[u], device_id={"dp": sibling})

    def send_term(u, k):
        return pltpu.make_async_remote_copy(
            red.at[u, lax.rem(row + k, n_y)], yrec.at[u, k - 1],
            y1s.at[u, k - 1], y1r.at[u, k - 1], device_id={"dp": y_peer(k)})

    def send_hidden(u, k):
        return pltpu.make_async_remote_copy(
            hid.at[u, core, row], hid.at[u, core, row],
            y2s.at[u, k - 1], y2r.at[u, k - 1], device_id={"dp": y_peer(k)})

    def send_group(u):
        return pltpu.make_async_remote_copy(
            hid.at[u, core], hid.at[u, core], s2s.at[u], s2r.at[u], device_id={"dp": sibling})

    for e in range(min(slots, n_exp)):
        for c in load_gu(e):
            c.start()
    for e in range(min(dslots, n_exp)):
        load_d(e).start()

    barrier = pltpu.get_barrier_semaphore()
    pl.semaphore_signal(barrier, inc=1, device_id={"dp": sibling})
    for k in range(1, n_y):
        pl.semaphore_signal(barrier, inc=1, device_id={"dp": y_peer(k)})
    pl.semaphore_wait(barrier, n_y)

    def onehot(e, at, size):
        rows = lax.broadcasted_iota(jnp.int32, (size, tok_count), 0) + at
        return rows == rank_ref[pl.ds(e, 1), :]

    def first(e):
        at = lax.rem(e, slots)
        for c in load_gu(e):
            c.wait()
        for r0, size in cut(full_rows, 128):
            x = jnp.dot(onehot(e, r0, size).astype(F32).astype(BF), tok_ref[...],
                        preferred_element_type=F32).astype(BF)
            for w, shift in ((wg, 0), (wu, ff)):
                for c0, width in cut(ff, 512):
                    p = jnp.dot(x, w[at, :, c0:c0 + width], preferred_element_type=F32).astype(BF)
                    cols = slice(shift + c0, shift + c0 + width)
                    step = min(size, unit // (CORES * n_y))
                    for r in range(0, size, step):
                        if r0 + r < base:
                            j = (r0 + r) // unit
                            left = (r0 + r) % unit
                            half = unit // CORES
                            part[e * per + j, left // half, (left % half) // step, :, cols] = p[r:r + step]
                    if spill and r0 + size > base:
                        lo = max(base - r0, 0)
                        over[pl.ds(pl.multiple_of(e * spill + r0 + lo - base, 16), size - lo), cols] = p[lo:]

        @pl.when(e + slots < n_exp)
        def _():
            for c in load_gu(e + slots):
                c.start()

        for j in range(per):
            send_half(e * per + j).start()

    def pooled():
        pick = (lax.broadcasted_iota(jnp.int32, (pool, n_exp * spill), 0) == prow_ref[...])
        pick = pick.astype(F32).astype(BF)
        for c0, width in cut(2 * ff, 512):
            p = jnp.dot(pick, over[:, c0:c0 + width], preferred_element_type=F32).astype(BF)
            part[n_exp * per:, :, :, :, c0:c0 + width] = p.reshape(
                (pool_units,) + part.shape[1:4] + (width,))
        for j in range(pool_units):
            send_half(n_exp * per + j).start()

    def second(u):
        send_half(u).wait_recv()
        for g in range(n_y):
            red[u, g] = (part[u, core, g].astype(F32) + sib[u, g].astype(F32)).astype(BF)
        for k in range(1, n_y):
            send_term(u, k).start()

    def third(u):
        for k in range(1, n_y):
            send_term(u, k).wait_recv()
        for c0, width in cut(ff, 512):
            g = red[u, row, :, c0:c0 + width].astype(F32)
            p = red[u, row, :, ff + c0:ff + c0 + width].astype(F32)
            for k in range(1, n_y):
                g += yrec[u, k - 1, :, c0:c0 + width].astype(F32)
                p += yrec[u, k - 1, :, ff + c0:ff + c0 + width].astype(F32)
            hid[u, core, row, :, c0:c0 + width] = (g / (1.0 + jnp.exp(-g)) * p).astype(BF)
        for k in range(1, n_y):
            send_hidden(u, k).start()

    def fourth(u):
        for k in range(1, n_y):
            send_hidden(u, k).wait_recv()
        send_group(u).start()

    lag_pair, lag_sum, lag_share = 1, 3, 5
    span = n_exp + (1 if pool else 0)

    def on_units(step, do):
        @pl.when((step >= 0) & (step < n_exp))
        def _():
            for j in range(per):
                do(step * per + j)
        if pool:
            @pl.when((step >= n_exp) & (step < n_exp + pool_units))
            def _():
                do(n_exp * per + step - n_exp)

    def step(s, carry):
        @pl.when(s < n_exp)
        def _():
            first(s)
        if pool:
            @pl.when(s == n_exp)
            def _():
                pooled()
        on_units(s - lag_pair, second)
        on_units(s - lag_sum, third)
        on_units(s - lag_share, fourth)
        return carry

    lax.fori_loop(0, n_exp + pool_units + lag_share, step, 0)

    if pool:
        def arrived(j, carry):
            send_group(n_exp * per + j).wait_recv()
            return carry
        lax.fori_loop(0, pool_units, arrived, 0)

    def down(e, carry):
        at = lax.rem(e, dslots)
        for j in range(per):
            send_group(e * per + j).wait_recv()
        load_d(e).wait()
        rows = hid[pl.ds(e * per, per)].reshape(base, ff)
        if spill:
            mine = pcol_ref[pl.ds(pl.multiple_of(e * spill, 16), spill), :]
            pick = (lax.broadcasted_iota(jnp.int32, (spill, pool), 1) == mine).astype(F32).astype(BF)
            more = jnp.dot(pick, hid[n_exp * per:].reshape(pool, ff), preferred_element_type=F32)
            rows = jnp.concatenate([rows, more.astype(BF)], axis=0)
        for c0, width in cut(db, 512):
            y = jnp.dot(rows, wd[at, :, c0:c0 + width], preferred_element_type=F32).astype(BF)
            eo[pl.ds(pl.multiple_of(e * full_rows, 16), full_rows), c0:c0 + width] = y
        for r0, size in cut(full_rows, 128):
            gmat[pl.ds(pl.multiple_of(e * full_rows + r0, 16), size), :] = jnp.where(
                onehot(e, r0, size), prob_ref[pl.ds(e, 1), :], 0.0).astype(BF)

        @pl.when(e + dslots < n_exp)
        def _():
            load_d(e + dslots).start()
        return carry

    lax.fori_loop(0, n_exp, down, 0)
    for t0, rows in cut(tok_count, 512):
        for c0, width in cut(db, 256):
            out_ref[t0:t0 + rows, c0:c0 + width] = lax.dot_general(
                gmat[:, t0:t0 + rows], eo[:, c0:c0 + width], (((0,), (0,)), ((), ())),
                preferred_element_type=F32).astype(BF)

    def drain(u, carry):
        send_half(u).wait_send()
        for k in range(1, n_y):
            send_term(u, k).wait_send()
            send_hidden(u, k).wait_send()
        send_group(u).wait_send()
        return carry

    lax.fori_loop(0, units, drain, 0)


def run_experts(n_dp, base, pool, full_rows, ident, tok, rank, prob, wg, wu, wd):
    n_exp, db, ff = wg.shape
    n_y = n_dp // CORES
    unit = 16 * n_dp
    units = (n_exp * base + pool) // unit
    spill = full_rows - base
    tok_count = tok.shape[0]
    slots, dslots = min(3, n_exp), min(4, n_exp)
    if spill:
        extra = jnp.maximum(jnp.max(rank, axis=1) + 1 - base, 0)
        start = jnp.cumsum(extra) - extra
        place = (start[:, None] + jnp.arange(spill, dtype=jnp.int32)[None, :]).reshape(-1)
    else:
        place = jnp.zeros((16,), jnp.int32)
    group = (CORES, n_y, 16)
    vm = pltpu.VMEM
    dma = pltpu.SemaphoreType.DMA
    inside = pl.BlockSpec(memory_space=pltpu.VMEM)
    outside = pl.BlockSpec(memory_space=pl.ANY)
    return pl.pallas_call(
        functools.partial(experts_kernel, n_y, base, pool, unit, full_rows),
        out_shape=jax.ShapeDtypeStruct((tok_count, db), BF),
        in_specs=[inside] * 5 + [outside] * 3,
        out_specs=inside,
        scratch_shapes=[
            vm((slots, db, ff), BF),
            vm((slots, db, ff), BF),
            vm((dslots, ff, db), BF),
            vm((units,) + group + (2 * ff,), BF),
            vm((n_exp * spill if spill else 16, 2 * ff), BF),
            vm((units, n_y, 16, 2 * ff), BF),
            vm((units, n_y, 16, 2 * ff), BF),
            vm((units, n_y - 1, 16, 2 * ff), BF),
            vm((units,) + group + (ff,), BF),
            vm((n_exp * full_rows, db), BF),
            vm((n_exp * full_rows, tok_count), BF),
            dma((slots,)), dma((slots,)), dma((dslots,)),
            dma((units,)), dma((units,)),
            dma((units, n_y - 1)), dma((units, n_y - 1)),
            dma((units, n_y - 1)), dma((units, n_y - 1)),
            dma((units,)), dma((units,)),
        ],
        compiler_params=pltpu.CompilerParams(
            collective_id=ident, has_side_effects=True, vmem_limit_bytes=61 * 1024 * 1024),
    )(tok, rank, prob, place.reshape(1, -1), place.reshape(-1, 1), wg, wu, wd)


def body(n_dp, tokens, routes, gate_probs, w_gate, w_up, w_down):
    group_tokens, top = routes.shape
    n_exp = w_gate.shape[0]
    names = ("tensor", "expert")
    owners = lax.axis_size("tensor") * lax.axis_size("expert")
    mine = lax.axis_index("tensor") * lax.axis_size("expert") + lax.axis_index("expert")
    full_rows = owners * (2 * group_tokens * top // (owners * n_exp))
    tok = lax.all_gather(tokens, names, axis=0, tiled=True)
    info = lax.all_gather(
        jnp.concatenate([routes.astype(F32), gate_probs], axis=1), names, axis=0, tiled=True)
    all_routes = info[:, :top].astype(jnp.int32)
    ids = mine * n_exp + jnp.arange(n_exp, dtype=jnp.int32)
    named = ids[:, None, None] == all_routes.T[None, :, :]
    chosen = jnp.any(named, axis=1)
    prob = jnp.sum(jnp.where(named, info[:, top:].T[None], 0.0), axis=1)
    count = all_routes.shape[0]
    before = lax.broadcasted_iota(jnp.int32, (count, count), 0) < lax.broadcasted_iota(
        jnp.int32, (count, count), 1)
    rank = jnp.dot(chosen.astype(BF), before.astype(BF), preferred_element_type=F32).astype(jnp.int32)
    rank = jnp.where(chosen, rank, -1)
    unit = 16 * n_dp
    args = (tok, rank, prob, w_gate, w_up, w_down)
    base, pool = full_rows // 2, n_exp * full_rows // 4
    if n_exp > 1 and base % unit == 0 and pool % unit == 0:
        everyone = jnp.arange(owners * n_exp, dtype=jnp.int32)
        loads = jnp.sum((all_routes.reshape(-1)[None, :] == everyone[:, None]).astype(jnp.int32), axis=1)
        extra = jnp.sum(jnp.maximum(loads - base, 0).reshape(owners, n_exp), axis=1)
        part = lax.cond(
            jnp.max(extra) <= pool,
            functools.partial(run_experts, n_dp, base, pool, full_rows, 1),
            functools.partial(run_experts, n_dp, full_rows, 0, full_rows, 2),
            *args)
    else:
        part = run_experts(n_dp, full_rows, 0, full_rows, 2, *args)
    back = lax.all_to_all(
        part.reshape(owners, group_tokens, -1), names, split_axis=0, concat_axis=0, tiled=True)
    return jnp.sum(back.astype(F32), axis=0).astype(BF)


def solution(mesh):
    placed = (
        P(("tensor", "expert"), "dp"),
        P(("tensor", "expert"), None),
        P(("tensor", "expert"), None),
        P(("tensor", "expert"), "dp", None),
        P(("tensor", "expert"), "dp", None),
        P(("tensor", "expert"), None, "dp"),
    )
    return jax.shard_map(
        functools.partial(body, mesh.shape["dp"]), mesh=mesh, in_specs=placed,
        out_specs=P(("tensor", "expert"), "dp"), check_vma=False
    )
```

```python
import functools

import jax
import jax.numpy as jnp
from jax import lax
from jax.experimental import pallas as pl
from jax.experimental.pallas import tpu as pltpu
from jax.sharding import PartitionSpec as P

BF = jnp.bfloat16
F32 = jnp.float32
CORES = 2


def cut(total, tile):
    return [(at, min(tile, total - at)) for at in range(0, total, tile)]


def gather_kernel(n_x, n_z, tok_ref, info_ref, tok_out, info_out, zs, zr, xs, xr):
    x, z = lax.axis_index("tensor"), lax.axis_index("expert")
    pairs = ((tok_ref, tok_out), (info_ref, info_out))

    def along_z(k, i):
        src, dst = pairs[i]
        return pltpu.make_async_remote_copy(
            src, dst.at[x * n_z + z], zs.at[k - 1, i], zr.at[k - 1, i],
            device_id={"expert": lax.rem(z + k, n_z)})

    def along_x(k, j, i):
        src, dst = pairs[i]
        block = x * n_z + lax.rem(z - k + n_z, n_z)
        return pltpu.make_async_remote_copy(
            src if k == 0 else dst.at[block], dst.at[block], xs.at[k, j - 1, i], xr.at[k, j - 1, i],
            device_id={"tensor": lax.rem(x + j, n_x)})

    barrier = pltpu.get_barrier_semaphore()
    for k in range(1, n_z):
        pl.semaphore_signal(barrier, inc=1, device_id={"expert": lax.rem(z + k, n_z)})
    for j in range(1, n_x):
        pl.semaphore_signal(barrier, inc=1, device_id={"tensor": lax.rem(x + j, n_x)})
    pl.semaphore_wait(barrier, n_z + n_x - 2)

    offsets = sorted(range(1, n_z), key=lambda k: min(k, n_z - k))
    for i in (1, 0):
        for j in range(1, n_x):
            along_x(0, j, i).start()
        for k in offsets:
            along_z(k, i).start()
    for src, dst in pairs:
        dst[x * n_z + z] = src[...]
    for i in (1, 0):
        for k in offsets:
            along_z(k, i).wait_recv()
            for j in range(1, n_x):
                along_x(k, j, i).start()
    for i in (1, 0):
        for k in range(n_z):
            for j in range(1, n_x):
                along_x(k, j, i).wait()
        for k in offsets:
            along_z(k, i).wait_send()


def gather_all(n_x, n_z, tokens, info):
    inside = pl.BlockSpec(memory_space=pltpu.VMEM)
    dma = pltpu.SemaphoreType.DMA
    owners = n_x * n_z
    return pl.pallas_call(
        functools.partial(gather_kernel, n_x, n_z),
        out_shape=[jax.ShapeDtypeStruct((owners,) + a.shape, a.dtype) for a in (tokens, info)],
        in_specs=[inside] * 2,
        out_specs=[inside] * 2,
        scratch_shapes=[
            dma((n_z - 1, 2)), dma((n_z - 1, 2)), dma((n_z, n_x - 1, 2)), dma((n_z, n_x - 1, 2))],
        compiler_params=pltpu.CompilerParams(
            collective_id=3, has_side_effects=True, vmem_limit_bytes=32 * 1024 * 1024),
    )(tokens, info)


def experts_kernel(
    n_y, n_x, n_z, base, pool, unit, full_rows,
    tok_ref, rank_ref, prob_ref, prow_ref, pcol_ref, wg_hbm, wu_hbm, wd_hbm,
    out_ref,
    wg, wu, wd, part, over, sib, red, yrec, hid, eo, gmat,
    pout, pown, xrec, zout, zrec,
    gsem, usem, dsem, s1s, s1r, y1s, y1r, y2s, y2r, s2s, s2r, xs, xr, zs, zr,
):
    n_exp, db, ff = wg_hbm.shape
    tok_count = tok_ref.shape[0]
    slots, dslots = wg.shape[0], wd.shape[0]
    per = base // unit
    units = part.shape[0]
    pool_units = pool // unit
    spill = full_rows - base
    me = lax.axis_index("dp")
    core = lax.rem(me, CORES)
    row = me // CORES
    sibling = row * CORES + (1 - core)
    x, z = lax.axis_index("tensor"), lax.axis_index("expert")
    block = tok_count // (n_x * n_z)

    def y_peer(k):
        return lax.rem(row + k, n_y) * CORES + core

    def load_gu(e):
        at = lax.rem(e, slots)
        return (
            pltpu.make_async_copy(wg_hbm.at[e], wg.at[at], gsem.at[at]),
            pltpu.make_async_copy(wu_hbm.at[e], wu.at[at], usem.at[at]),
        )

    def load_d(e):
        at = lax.rem(e, dslots)
        return pltpu.make_async_copy(wd_hbm.at[e], wd.at[at], dsem.at[at])

    def send_half(u):
        return pltpu.make_async_remote_copy(
            part.at[u, 1 - core], sib.at[u], s1s.at[u], s1r.at[u], device_id={"dp": sibling})

    def send_term(u, k):
        return pltpu.make_async_remote_copy(
            red.at[u, lax.rem(row + k, n_y)], yrec.at[u, k - 1],
            y1s.at[u, k - 1], y1r.at[u, k - 1], device_id={"dp": y_peer(k)})

    def send_hidden(u, k):
        return pltpu.make_async_remote_copy(
            hid.at[u, core, row], hid.at[u, core, row],
            y2s.at[u, k - 1], y2r.at[u, k - 1], device_id={"dp": y_peer(k)})

    def send_group(u):
        return pltpu.make_async_remote_copy(
            hid.at[u, core], hid.at[u, core], s2s.at[u], s2r.at[u], device_id={"dp": sibling})

    def send_x(j, zz):
        there = lax.rem(x + j, n_x)
        return pltpu.make_async_remote_copy(
            pout.at[j - 1, zz], xrec.at[j - 1, zz], xs.at[j - 1, zz], xr.at[j - 1, zz],
            device_id={"tensor": there})

    def send_z(k):
        zz = lax.rem(z + k, n_z)
        return pltpu.make_async_remote_copy(
            zout.at[k - 1], zrec.at[k - 1], zs.at[k - 1], zr.at[k - 1], device_id={"expert": zz})

    for e in range(min(slots, n_exp)):
        for c in load_gu(e):
            c.start()
    for e in range(min(dslots, n_exp)):
        load_d(e).start()

    barrier = pltpu.get_barrier_semaphore()
    pl.semaphore_signal(barrier, inc=1, device_id={"dp": sibling})
    for k in range(1, n_y):
        pl.semaphore_signal(barrier, inc=1, device_id={"dp": y_peer(k)})
    for j in range(1, n_x):
        pl.semaphore_signal(barrier, inc=1, device_id={"tensor": lax.rem(x + j, n_x)})
    for k in range(1, n_z):
        pl.semaphore_signal(barrier, inc=1, device_id={"expert": lax.rem(z + k, n_z)})
    pl.semaphore_wait(barrier, n_y + n_x + n_z - 2)

    def onehot(e, at, size):
        rows = lax.broadcasted_iota(jnp.int32, (size, tok_count), 0) + at
        return rows == rank_ref[pl.ds(e, 1), :]

    def first(e):
        at = lax.rem(e, slots)
        for c in load_gu(e):
            c.wait()
        for r0, size in cut(full_rows, 128):
            x = jnp.dot(onehot(e, r0, size).astype(F32).astype(BF), tok_ref[...],
                        preferred_element_type=F32).astype(BF)
            for w, shift in ((wg, 0), (wu, ff)):
                for c0, width in cut(ff, 512):
                    p = jnp.dot(x, w[at, :, c0:c0 + width], preferred_element_type=F32).astype(BF)
                    cols = slice(shift + c0, shift + c0 + width)
                    step = min(size, unit // (CORES * n_y))
                    for r in range(0, size, step):
                        if r0 + r < base:
                            j = (r0 + r) // unit
                            left = (r0 + r) % unit
                            half = unit // CORES
                            part[e * per + j, left // half, (left % half) // step, :, cols] = p[r:r + step]
                    if spill and r0 + size > base:
                        lo = max(base - r0, 0)
                        over[pl.ds(pl.multiple_of(e * spill + r0 + lo - base, 16), size - lo), cols] = p[lo:]

        @pl.when(e + slots < n_exp)
        def _():
            for c in load_gu(e + slots):
                c.start()

        for j in range(per):
            send_half(e * per + j).start()

    def pooled():
        pick = (lax.broadcasted_iota(jnp.int32, (pool, n_exp * spill), 0) == prow_ref[...])
        pick = pick.astype(F32).astype(BF)
        for c0, width in cut(2 * ff, 512):
            p = jnp.dot(pick, over[:, c0:c0 + width], preferred_element_type=F32).astype(BF)
            part[n_exp * per:, :, :, :, c0:c0 + width] = p.reshape(
                (pool_units,) + part.shape[1:4] + (width,))
        for j in range(pool_units):
            send_half(n_exp * per + j).start()

    def second(u):
        send_half(u).wait_recv()
        for g in range(n_y):
            red[u, g] = (part[u, core, g].astype(F32) + sib[u, g].astype(F32)).astype(BF)
        for k in range(1, n_y):
            send_term(u, k).start()

    def third(u):
        for k in range(1, n_y):
            send_term(u, k).wait_recv()
        for c0, width in cut(ff, 512):
            g = red[u, row, :, c0:c0 + width].astype(F32)
            p = red[u, row, :, ff + c0:ff + c0 + width].astype(F32)
            for k in range(1, n_y):
                g += yrec[u, k - 1, :, c0:c0 + width].astype(F32)
                p += yrec[u, k - 1, :, ff + c0:ff + c0 + width].astype(F32)
            hid[u, core, row, :, c0:c0 + width] = (g / (1.0 + jnp.exp(-g)) * p).astype(BF)
        for k in range(1, n_y):
            send_hidden(u, k).start()

    def fourth(u):
        for k in range(1, n_y):
            send_hidden(u, k).wait_recv()
        send_group(u).start()

    lag_pair, lag_sum, lag_share = 1, 3, 5

    def on_units(step, do):
        @pl.when((step >= 0) & (step < n_exp))
        def _():
            for j in range(per):
                do(step * per + j)
        if pool:
            @pl.when((step >= n_exp) & (step < n_exp + pool_units))
            def _():
                do(n_exp * per + step - n_exp)

    def step(s, carry):
        @pl.when(s < n_exp)
        def _():
            first(s)
        if pool:
            @pl.when(s == n_exp)
            def _():
                pooled()
        on_units(s - lag_pair, second)
        on_units(s - lag_sum, third)
        on_units(s - lag_share, fourth)
        return carry

    lax.fori_loop(0, n_exp + pool_units + lag_share, step, 0)

    if pool:
        def arrived(j, carry):
            send_group(n_exp * per + j).wait_recv()
            return carry
        lax.fori_loop(0, pool_units, arrived, 0)

    def down(e, carry):
        at = lax.rem(e, dslots)
        for j in range(per):
            send_group(e * per + j).wait_recv()
        load_d(e).wait()
        rows = hid[pl.ds(e * per, per)].reshape(base, ff)
        if spill:
            mine = pcol_ref[pl.ds(pl.multiple_of(e * spill, 16), spill), :]
            pick = (lax.broadcasted_iota(jnp.int32, (spill, pool), 1) == mine).astype(F32).astype(BF)
            more = jnp.dot(pick, hid[n_exp * per:].reshape(pool, ff), preferred_element_type=F32)
            rows = jnp.concatenate([rows, more.astype(BF)], axis=0)
        for c0, width in cut(db, 512):
            y = jnp.dot(rows, wd[at, :, c0:c0 + width], preferred_element_type=F32).astype(BF)
            eo[pl.ds(pl.multiple_of(e * full_rows, 16), full_rows), c0:c0 + width] = y
        for r0, size in cut(full_rows, 128):
            gmat[pl.ds(pl.multiple_of(e * full_rows + r0, 16), size), :] = jnp.where(
                onehot(e, r0, size), prob_ref[pl.ds(e, 1), :], 0.0).astype(BF)

        @pl.when(e + dslots < n_exp)
        def _():
            load_d(e + dslots).start()
        return carry

    lax.fori_loop(0, n_exp, down, 0)
    span = n_z * block
    far = sorted(range(1, n_z), key=lambda k: -min(k, n_z - k))

    def combine(j, c0, width):
        at = pl.multiple_of(lax.rem(x + j, n_x) * span, span)
        y = lax.dot_general(
            gmat[:, pl.ds(at, span)], eo[:, c0:c0 + width], (((0,), (0,)), ((), ())),
            preferred_element_type=F32)
        return y.reshape(n_z, block, width)

    for j in range(1, n_x):
        for c0, width in cut(db, 512):
            pout[j - 1, :, :, c0:c0 + width] = combine(j, c0, width).astype(BF)
        for k in far + [0]:
            send_x(j, lax.rem(z + k, n_z)).start()
    for c0, width in cut(db, 512):
        pown[:, :, c0:c0 + width] = combine(0, c0, width)

    for k in far + [0]:
        zz = lax.rem(z + k, n_z)
        mine = pown[zz]
        for j in range(1, n_x):
            send_x(j, zz).wait_recv()
            mine += xrec[j - 1, zz].astype(F32)
        if k:
            zout[k - 1] = mine.astype(BF)
            send_z(k).start()
        else:
            pown[zz] = mine
    total = pown[z]
    for k in far[::-1]:
        send_z(k).wait_recv()
        total += zrec[k - 1].astype(F32)
    out_ref[...] = total.astype(BF)
    for k in far:
        send_z(k).wait_send()
    for j in range(1, n_x):
        for k in range(n_z):
            send_x(j, k).wait_send()

    def drain(u, carry):
        send_half(u).wait_send()
        for k in range(1, n_y):
            send_term(u, k).wait_send()
            send_hidden(u, k).wait_send()
        send_group(u).wait_send()
        return carry

    lax.fori_loop(0, units, drain, 0)


def run_experts(n_dp, n_x, n_z, base, pool, full_rows, ident, tok, rank, prob, wg, wu, wd):
    n_exp, db, ff = wg.shape
    n_y = n_dp // CORES
    unit = 16 * n_dp
    units = (n_exp * base + pool) // unit
    spill = full_rows - base
    tok_count = tok.shape[0]
    block = tok_count // (n_x * n_z)
    slots, dslots = min(3, n_exp), min(4, n_exp)
    if spill:
        extra = jnp.maximum(jnp.max(rank, axis=1) + 1 - base, 0)
        start = jnp.cumsum(extra) - extra
        place = (start[:, None] + jnp.arange(spill, dtype=jnp.int32)[None, :]).reshape(-1)
    else:
        place = jnp.zeros((16,), jnp.int32)
    group = (CORES, n_y, 16)
    vm = pltpu.VMEM
    dma = pltpu.SemaphoreType.DMA
    inside = pl.BlockSpec(memory_space=pltpu.VMEM)
    outside = pl.BlockSpec(memory_space=pl.ANY)
    return pl.pallas_call(
        functools.partial(experts_kernel, n_y, n_x, n_z, base, pool, unit, full_rows),
        out_shape=jax.ShapeDtypeStruct((block, db), BF),
        in_specs=[inside] * 5 + [outside] * 3,
        out_specs=inside,
        scratch_shapes=[
            vm((slots, db, ff), BF),
            vm((slots, db, ff), BF),
            vm((dslots, ff, db), BF),
            vm((units,) + group + (2 * ff,), BF),
            vm((n_exp * spill if spill else 16, 2 * ff), BF),
            vm((units, n_y, 16, 2 * ff), BF),
            vm((units, n_y, 16, 2 * ff), BF),
            vm((units, n_y - 1, 16, 2 * ff), BF),
            vm((units,) + group + (ff,), BF),
            vm((n_exp * full_rows, db), BF),
            vm((n_exp * full_rows, tok_count), BF),
            vm((n_x - 1, n_z, block, db), BF),
            vm((n_z, block, db), F32),
            vm((n_x - 1, n_z, block, db), BF),
            vm((n_z - 1, block, db), BF),
            vm((n_z - 1, block, db), BF),
            dma((slots,)), dma((slots,)), dma((dslots,)),
            dma((units,)), dma((units,)),
            dma((units, n_y - 1)), dma((units, n_y - 1)),
            dma((units, n_y - 1)), dma((units, n_y - 1)),
            dma((units,)), dma((units,)),
            dma((n_x - 1, n_z)), dma((n_x - 1, n_z)), dma((n_z - 1,)), dma((n_z - 1,)),
        ],
        compiler_params=pltpu.CompilerParams(
            collective_id=ident, has_side_effects=True, vmem_limit_bytes=61 * 1024 * 1024),
    )(tok, rank, prob, place.reshape(1, -1), place.reshape(-1, 1), wg, wu, wd)


def body(n_dp, tokens, routes, gate_probs, w_gate, w_up, w_down):
    group_tokens, top = routes.shape
    n_exp = w_gate.shape[0]
    n_x, n_z = lax.axis_size("tensor"), lax.axis_size("expert")
    owners = n_x * n_z
    mine = lax.axis_index("tensor") * n_z + lax.axis_index("expert")
    full_rows = owners * (2 * group_tokens * top // (owners * n_exp))
    info = jnp.concatenate([routes.astype(F32), gate_probs], axis=1).T
    tok, info = gather_all(n_x, n_z, tokens, info)
    tok = tok.reshape(owners * group_tokens, -1)
    info = info.transpose(0, 2, 1).reshape(owners * group_tokens, 2 * top)
    all_routes = info[:, :top].astype(jnp.int32)
    ids = mine * n_exp + jnp.arange(n_exp, dtype=jnp.int32)
    named = ids[:, None, None] == all_routes.T[None, :, :]
    chosen = jnp.any(named, axis=1)
    prob = jnp.sum(jnp.where(named, info[:, top:].T[None], 0.0), axis=1)
    count = all_routes.shape[0]
    before = lax.broadcasted_iota(jnp.int32, (count, count), 0) < lax.broadcasted_iota(
        jnp.int32, (count, count), 1)
    rank = jnp.dot(chosen.astype(BF), before.astype(BF), preferred_element_type=F32).astype(jnp.int32)
    rank = jnp.where(chosen, rank, -1)
    unit = 16 * n_dp
    args = (tok, rank, prob, w_gate, w_up, w_down)
    base, pool = full_rows // 2, n_exp * full_rows // 4
    if n_exp > 1 and base % unit == 0 and pool % unit == 0:
        everyone = jnp.arange(owners * n_exp, dtype=jnp.int32)
        loads = jnp.sum((all_routes.reshape(-1)[None, :] == everyone[:, None]).astype(jnp.int32), axis=1)
        extra = jnp.sum(jnp.maximum(loads - base, 0).reshape(owners, n_exp), axis=1)
        part = lax.cond(
            jnp.max(extra) <= pool,
            functools.partial(run_experts, n_dp, n_x, n_z, base, pool, full_rows, 1),
            functools.partial(run_experts, n_dp, n_x, n_z, full_rows, 0, full_rows, 2),
            *args)
    else:
        part = run_experts(n_dp, n_x, n_z, full_rows, 0, full_rows, 2, *args)
    return part


def solution(mesh):
    placed = (
        P(("tensor", "expert"), "dp"),
        P(("tensor", "expert"), None),
        P(("tensor", "expert"), None),
        P(("tensor", "expert"), "dp", None),
        P(("tensor", "expert"), "dp", None),
        P(("tensor", "expert"), None, "dp"),
    )
    return jax.shard_map(
        functools.partial(body, mesh.shape["dp"]), mesh=mesh, in_specs=placed,
        out_specs=P(("tensor", "expert"), "dp"), check_vma=False
    )
```

```python
import functools

import jax
import jax.numpy as jnp
from jax import lax
from jax.experimental import pallas as pl
from jax.experimental.pallas import tpu as pltpu
from jax.sharding import PartitionSpec as P

BF = jnp.bfloat16
F32 = jnp.float32
CORES = 2


def cut(total, tile):
    return [(at, min(tile, total - at)) for at in range(0, total, tile)]


def gather_kernel(n_x, n_z, tok_ref, info_ref, tok_out, info_out, zs, zr, xs, xr):
    x, z = lax.axis_index("tensor"), lax.axis_index("expert")
    pairs = ((tok_ref, tok_out), (info_ref, info_out))

    def along_z(k, i):
        src, dst = pairs[i]
        return pltpu.make_async_remote_copy(
            src, dst.at[x * n_z + z], zs.at[k - 1, i], zr.at[k - 1, i],
            device_id={"expert": lax.rem(z + k, n_z)})

    def along_x(k, j, i):
        src, dst = pairs[i]
        block = x * n_z + lax.rem(z - k + n_z, n_z)
        return pltpu.make_async_remote_copy(
            src if k == 0 else dst.at[block], dst.at[block], xs.at[k, j - 1, i], xr.at[k, j - 1, i],
            device_id={"tensor": lax.rem(x + j, n_x)})

    barrier = pltpu.get_barrier_semaphore()
    for k in range(1, n_z):
        pl.semaphore_signal(barrier, inc=1, device_id={"expert": lax.rem(z + k, n_z)})
    for j in range(1, n_x):
        pl.semaphore_signal(barrier, inc=1, device_id={"tensor": lax.rem(x + j, n_x)})
    pl.semaphore_wait(barrier, n_z + n_x - 2)

    offsets = sorted(range(1, n_z), key=lambda k: min(k, n_z - k))
    for i in (1, 0):
        for j in range(1, n_x):
            along_x(0, j, i).start()
        for k in offsets:
            along_z(k, i).start()
    for src, dst in pairs:
        dst[x * n_z + z] = src[...]
    for i in (1, 0):
        for k in offsets:
            along_z(k, i).wait_recv()
            for j in range(1, n_x):
                along_x(k, j, i).start()
    for i in (1, 0):
        for k in range(n_z):
            for j in range(1, n_x):
                along_x(k, j, i).wait()
        for k in offsets:
            along_z(k, i).wait_send()


def gather_all(n_x, n_z, tokens, info):
    inside = pl.BlockSpec(memory_space=pltpu.VMEM)
    dma = pltpu.SemaphoreType.DMA
    owners = n_x * n_z
    return pl.pallas_call(
        functools.partial(gather_kernel, n_x, n_z),
        out_shape=[jax.ShapeDtypeStruct((owners,) + a.shape, a.dtype) for a in (tokens, info)],
        in_specs=[inside] * 2,
        out_specs=[inside] * 2,
        scratch_shapes=[
            dma((n_z - 1, 2)), dma((n_z - 1, 2)), dma((n_z, n_x - 1, 2)), dma((n_z, n_x - 1, 2))],
        compiler_params=pltpu.CompilerParams(
            collective_id=3, has_side_effects=True, vmem_limit_bytes=32 * 1024 * 1024),
    )(tokens, info)


def experts_kernel(
    n_y, n_x, n_z, base, pool, unit, full_rows,
    tok_ref, rank_ref, prob_ref, prow_ref, pcol_ref, wg_hbm, wu_hbm, wd_hbm,
    out_ref,
    wg, wu, wd, part, over, sib, red, yrec, hid, eo, gmat,
    pout, pown, xrec, zout, zrec,
    gsem, usem, dsem, s1s, s1r, y1s, y1r, y2s, y2r, s2s, s2r, xs, xr, zs, zr,
):
    n_exp, db, ff = wg_hbm.shape
    tok_count = tok_ref.shape[0]
    slots = wg.shape[0]
    per = base // unit
    units = part.shape[0]
    pool_units = pool // unit
    spill = full_rows - base
    me = lax.axis_index("dp")
    core = lax.rem(me, CORES)
    row = me // CORES
    sibling = row * CORES + (1 - core)
    x, z = lax.axis_index("tensor"), lax.axis_index("expert")
    block = tok_count // (n_x * n_z)

    def y_peer(k):
        return lax.rem(row + k, n_y) * CORES + core

    def load_gu(e):
        at = lax.rem(e, slots)
        return (
            pltpu.make_async_copy(wg_hbm.at[e], wg.at[at], gsem.at[at]),
            pltpu.make_async_copy(wu_hbm.at[e], wu.at[at], usem.at[at]),
        )

    def load_d(e):
        return pltpu.make_async_copy(wd_hbm.at[e], wd.at[e], dsem.at[e])

    def send_half(u):
        return pltpu.make_async_remote_copy(
            part.at[u, 1 - core], sib.at[u], s1s.at[u], s1r.at[u], device_id={"dp": sibling})

    def send_term(u, k):
        return pltpu.make_async_remote_copy(
            red.at[u, lax.rem(row + k, n_y)], yrec.at[u, k - 1],
            y1s.at[u, k - 1], y1r.at[u, k - 1], device_id={"dp": y_peer(k)})

    def send_hidden(u, k):
        return pltpu.make_async_remote_copy(
            hid.at[u, core, row], hid.at[u, core, row],
            y2s.at[u, k - 1], y2r.at[u, k - 1], device_id={"dp": y_peer(k)})

    def send_group(u):
        return pltpu.make_async_remote_copy(
            hid.at[u, core], hid.at[u, core], s2s.at[u], s2r.at[u], device_id={"dp": sibling})

    def send_x(h, j, zz):
        there = lax.rem(x + j, n_x)
        return pltpu.make_async_remote_copy(
            pout.at[h, j - 1, zz], xrec.at[h, j - 1, zz], xs.at[h, j - 1, zz], xr.at[h, j - 1, zz],
            device_id={"tensor": there})

    def send_z(h, k):
        zz = lax.rem(z + k, n_z)
        return pltpu.make_async_remote_copy(
            zout.at[h, k - 1], zrec.at[h, k - 1], zs.at[h, k - 1], zr.at[h, k - 1], device_id={"expert": zz})

    for e in range(min(slots, n_exp)):
        for c in load_gu(e):
            c.start()

    barrier = pltpu.get_barrier_semaphore()
    pl.semaphore_signal(barrier, inc=1, device_id={"dp": sibling})
    for k in range(1, n_y):
        pl.semaphore_signal(barrier, inc=1, device_id={"dp": y_peer(k)})
    for j in range(1, n_x):
        pl.semaphore_signal(barrier, inc=1, device_id={"tensor": lax.rem(x + j, n_x)})
    for k in range(1, n_z):
        pl.semaphore_signal(barrier, inc=1, device_id={"expert": lax.rem(z + k, n_z)})
    pl.semaphore_wait(barrier, n_y + n_x + n_z - 2)

    def onehot(e, at, size):
        rows = lax.broadcasted_iota(jnp.int32, (size, tok_count), 0) + at
        return rows == rank_ref[pl.ds(e, 1), :]

    def first(e):
        at = lax.rem(e, slots)
        for c in load_gu(e):
            c.wait()
        for r0, size in cut(full_rows, 128):
            x = jnp.dot(onehot(e, r0, size).astype(F32).astype(BF), tok_ref[...],
                        preferred_element_type=F32).astype(BF)
            for w, shift in ((wg, 0), (wu, ff)):
                for c0, width in cut(ff, 512):
                    p = jnp.dot(x, w[at, :, c0:c0 + width], preferred_element_type=F32).astype(BF)
                    cols = slice(shift + c0, shift + c0 + width)
                    step = min(size, unit // (CORES * n_y))
                    for r in range(0, size, step):
                        if r0 + r < base:
                            j = (r0 + r) // unit
                            left = (r0 + r) % unit
                            half = unit // CORES
                            part[e * per + j, left // half, (left % half) // step, :, cols] = p[r:r + step]
                    if spill and r0 + size > base:
                        lo = max(base - r0, 0)
                        over[pl.ds(pl.multiple_of(e * spill + r0 + lo - base, 16), size - lo), cols] = p[lo:]

        @pl.when(e + slots < n_exp)
        def _():
            for c in load_gu(e + slots):
                c.start()

        load_d(e).start()
        for j in range(per):
            send_half(e * per + j).start()

    def pooled():
        pick = (lax.broadcasted_iota(jnp.int32, (pool, n_exp * spill), 0) == prow_ref[...])
        pick = pick.astype(F32).astype(BF)
        for c0, width in cut(2 * ff, 512):
            p = jnp.dot(pick, over[:, c0:c0 + width], preferred_element_type=F32).astype(BF)
            part[n_exp * per:, :, :, :, c0:c0 + width] = p.reshape(
                (pool_units,) + part.shape[1:4] + (width,))
        for j in range(pool_units):
            send_half(n_exp * per + j).start()

    def second(u):
        send_half(u).wait_recv()
        for g in range(n_y):
            red[u, g] = (part[u, core, g].astype(F32) + sib[u, g].astype(F32)).astype(BF)
        for k in range(1, n_y):
            send_term(u, k).start()

    def third(u):
        for k in range(1, n_y):
            send_term(u, k).wait_recv()
        for c0, width in cut(ff, 512):
            g = red[u, row, :, c0:c0 + width].astype(F32)
            p = red[u, row, :, ff + c0:ff + c0 + width].astype(F32)
            for k in range(1, n_y):
                g += yrec[u, k - 1, :, c0:c0 + width].astype(F32)
                p += yrec[u, k - 1, :, ff + c0:ff + c0 + width].astype(F32)
            hid[u, core, row, :, c0:c0 + width] = (g / (1.0 + jnp.exp(-g)) * p).astype(BF)
        for k in range(1, n_y):
            send_hidden(u, k).start()

    def fourth(u):
        for k in range(1, n_y):
            send_hidden(u, k).wait_recv()
        send_group(u).start()

    lag_pair, lag_sum, lag_share = 1, 3, 5

    def on_units(step, do):
        @pl.when((step >= 0) & (step < n_exp))
        def _():
            for j in range(per):
                do(step * per + j)
        if pool:
            @pl.when((step >= n_exp) & (step < n_exp + pool_units))
            def _():
                do(n_exp * per + step - n_exp)

    def step(s, carry):
        @pl.when(s < n_exp)
        def _():
            first(s)
        if pool:
            @pl.when(s == n_exp)
            def _():
                pooled()
        on_units(s - lag_pair, second)
        on_units(s - lag_sum, third)
        on_units(s - lag_share, fourth)
        return carry

    lax.fori_loop(0, n_exp + pool_units + lag_share, step, 0)

    if pool:
        def arrived(j, carry):
            send_group(n_exp * per + j).wait_recv()
            return carry
        lax.fori_loop(0, pool_units, arrived, 0)

    def ready(e, carry):
        for j in range(per):
            send_group(e * per + j).wait_recv()
        load_d(e).wait()
        if spill:
            mine = pcol_ref[pl.ds(pl.multiple_of(e * spill, 16), spill), :]
            pick = (lax.broadcasted_iota(jnp.int32, (spill, pool), 1) == mine).astype(F32).astype(BF)
            more = jnp.dot(pick, hid[n_exp * per:].reshape(pool, ff), preferred_element_type=F32)
            over[pl.ds(pl.multiple_of(e * spill, 16), spill), :ff] = more.astype(BF)
        for r0, size in cut(full_rows, 128):
            gmat[pl.ds(pl.multiple_of(e * full_rows + r0, 16), size), :] = jnp.where(
                onehot(e, r0, size), prob_ref[pl.ds(e, 1), :], 0.0).astype(BF)
        return carry

    lax.fori_loop(0, n_exp, ready, 0)

    halves = cut(db, db // 2)
    part_span = n_z * block
    far = sorted(range(1, n_z), key=lambda k: -min(k, n_z - k))

    def combine(j, c0, width):
        at = pl.multiple_of(lax.rem(x + j, n_x) * part_span, part_span)
        y = lax.dot_general(
            gmat[:, pl.ds(at, part_span)], eo[:, c0:c0 + width], (((0,), (0,)), ((), ())),
            preferred_element_type=F32)
        return y.reshape(n_z, block, width)

    for h, (c0, width) in enumerate(halves):
        def down(e, carry, c0=c0, width=width):
            rows = hid[pl.ds(e * per, per)].reshape(base, ff)
            if spill:
                more = over[pl.ds(pl.multiple_of(e * spill, 16), spill), :ff]
                rows = jnp.concatenate([rows, more], axis=0)
            y = jnp.dot(rows, wd[e, :, c0:c0 + width], preferred_element_type=F32).astype(BF)
            eo[pl.ds(pl.multiple_of(e * full_rows, 16), full_rows), c0:c0 + width] = y
            return carry

        lax.fori_loop(0, n_exp, down, 0)
        for j in range(1, n_x):
            pout[h, j - 1] = combine(j, c0, width).astype(BF)
            for k in far + [0]:
                send_x(h, j, lax.rem(z + k, n_z)).start()
        pown[h] = combine(0, c0, width)

    for h in range(len(halves)):
        for k in far + [0]:
            zz = lax.rem(z + k, n_z)
            mine = pown[h, zz]
            for j in range(1, n_x):
                send_x(h, j, zz).wait_recv()
                mine += xrec[h, j - 1, zz].astype(F32)
            if k:
                zout[h, k - 1] = mine.astype(BF)
                send_z(h, k).start()
            else:
                pown[h, zz] = mine
    for h, (c0, width) in enumerate(halves):
        total = pown[h, z]
        for k in far[::-1]:
            send_z(h, k).wait_recv()
            total += zrec[h, k - 1].astype(F32)
        out_ref[:, c0:c0 + width] = total.astype(BF)
    for h in range(len(halves)):
        for k in far:
            send_z(h, k).wait_send()
        for j in range(1, n_x):
            for k in range(n_z):
                send_x(h, j, k).wait_send()

    def drain(u, carry):
        send_half(u).wait_send()
        for k in range(1, n_y):
            send_term(u, k).wait_send()
            send_hidden(u, k).wait_send()
        send_group(u).wait_send()
        return carry

    lax.fori_loop(0, units, drain, 0)


def run_experts(n_dp, n_x, n_z, base, pool, full_rows, ident, tok, rank, prob, wg, wu, wd):
    n_exp, db, ff = wg.shape
    n_y = n_dp // CORES
    unit = 16 * n_dp
    units = (n_exp * base + pool) // unit
    spill = full_rows - base
    tok_count = tok.shape[0]
    block = tok_count // (n_x * n_z)
    slots, dslots = min(2, n_exp), n_exp
    if spill:
        extra = jnp.maximum(jnp.max(rank, axis=1) + 1 - base, 0)
        start = jnp.cumsum(extra) - extra
        place = (start[:, None] + jnp.arange(spill, dtype=jnp.int32)[None, :]).reshape(-1)
    else:
        place = jnp.zeros((16,), jnp.int32)
    group = (CORES, n_y, 16)
    vm = pltpu.VMEM
    dma = pltpu.SemaphoreType.DMA
    inside = pl.BlockSpec(memory_space=pltpu.VMEM)
    outside = pl.BlockSpec(memory_space=pl.ANY)
    return pl.pallas_call(
        functools.partial(experts_kernel, n_y, n_x, n_z, base, pool, unit, full_rows),
        out_shape=jax.ShapeDtypeStruct((block, db), BF),
        in_specs=[inside] * 5 + [outside] * 3,
        out_specs=inside,
        scratch_shapes=[
            vm((slots, db, ff), BF),
            vm((slots, db, ff), BF),
            vm((dslots, ff, db), BF),
            vm((units,) + group + (2 * ff,), BF),
            vm((n_exp * spill if spill else 16, 2 * ff), BF),
            vm((units, n_y, 16, 2 * ff), BF),
            vm((units, n_y, 16, 2 * ff), BF),
            vm((units, n_y - 1, 16, 2 * ff), BF),
            vm((units,) + group + (ff,), BF),
            vm((n_exp * full_rows, db), BF),
            vm((n_exp * full_rows, tok_count), BF),
            vm((2, n_x - 1, n_z, block, db // 2), BF),
            vm((2, n_z, block, db // 2), F32),
            vm((2, n_x - 1, n_z, block, db // 2), BF),
            vm((2, n_z - 1, block, db // 2), BF),
            vm((2, n_z - 1, block, db // 2), BF),
            dma((slots,)), dma((slots,)), dma((dslots,)),
            dma((units,)), dma((units,)),
            dma((units, n_y - 1)), dma((units, n_y - 1)),
            dma((units, n_y - 1)), dma((units, n_y - 1)),
            dma((units,)), dma((units,)),
            dma((2, n_x - 1, n_z)), dma((2, n_x - 1, n_z)), dma((2, n_z - 1)), dma((2, n_z - 1)),
        ],
        compiler_params=pltpu.CompilerParams(
            collective_id=ident, has_side_effects=True, vmem_limit_bytes=61 * 1024 * 1024),
    )(tok, rank, prob, place.reshape(1, -1), place.reshape(-1, 1), wg, wu, wd)


def body(n_dp, tokens, routes, gate_probs, w_gate, w_up, w_down):
    group_tokens, top = routes.shape
    n_exp = w_gate.shape[0]
    n_x, n_z = lax.axis_size("tensor"), lax.axis_size("expert")
    owners = n_x * n_z
    mine = lax.axis_index("tensor") * n_z + lax.axis_index("expert")
    full_rows = owners * (2 * group_tokens * top // (owners * n_exp))
    info = jnp.concatenate([routes.astype(F32), gate_probs], axis=1).T
    tok, info = gather_all(n_x, n_z, tokens, info)
    tok = tok.reshape(owners * group_tokens, -1)
    info = info.transpose(0, 2, 1).reshape(owners * group_tokens, 2 * top)
    all_routes = info[:, :top].astype(jnp.int32)
    ids = mine * n_exp + jnp.arange(n_exp, dtype=jnp.int32)
    named = ids[:, None, None] == all_routes.T[None, :, :]
    chosen = jnp.any(named, axis=1)
    prob = jnp.sum(jnp.where(named, info[:, top:].T[None], 0.0), axis=1)
    count = all_routes.shape[0]
    before = lax.broadcasted_iota(jnp.int32, (count, count), 0) < lax.broadcasted_iota(
        jnp.int32, (count, count), 1)
    rank = jnp.dot(chosen.astype(BF), before.astype(BF), preferred_element_type=F32).astype(jnp.int32)
    rank = jnp.where(chosen, rank, -1)
    unit = 16 * n_dp
    args = (tok, rank, prob, w_gate, w_up, w_down)
    base, quarter = full_rows // 2, n_exp * full_rows // 16
    if n_exp > 1 and base % unit == 0 and quarter % unit == 0:
        everyone = jnp.arange(owners * n_exp, dtype=jnp.int32)
        loads = jnp.sum((all_routes.reshape(-1)[None, :] == everyone[:, None]).astype(jnp.int32), axis=1)
        extra = jnp.sum(jnp.maximum(loads - base, 0).reshape(owners, n_exp), axis=1)
        most = jnp.max(extra)
        pools = (3 * quarter, 4 * quarter)
        level = sum((most > p).astype(jnp.int32) for p in pools)
        part = lax.switch(
            level,
            [functools.partial(run_experts, n_dp, n_x, n_z, base, p, full_rows, 4 + i)
             for i, p in enumerate(pools)]
            + [functools.partial(run_experts, n_dp, n_x, n_z, full_rows, 0, full_rows, 2)],
            *args)
    else:
        part = run_experts(n_dp, n_x, n_z, full_rows, 0, full_rows, 2, *args)
    return part


def solution(mesh):
    placed = (
        P(("tensor", "expert"), "dp"),
        P(("tensor", "expert"), None),
        P(("tensor", "expert"), None),
        P(("tensor", "expert"), "dp", None),
        P(("tensor", "expert"), "dp", None),
        P(("tensor", "expert"), None, "dp"),
    )
    return jax.shard_map(
        functools.partial(body, mesh.shape["dp"]), mesh=mesh, in_specs=placed,
        out_specs=P(("tensor", "expert"), "dp"), check_vma=False
    )
```
